32 devices in a mesh: task: 2 (over y), shard: 16 (over z, x, core).
Axes of the slice: x: 2, y: 2, z: 4, core: 2. Of those that a mesh axis runs over, the one named last changes fastest.
Arguments:
- acts: bfloat16 [2, 1024, 4096], P('task', 'shard'), may hold values from -6 to 6
- cotangents: bfloat16 [2, 1024, 16384], P('task', 'shard'), may hold values from -0.75 to 0.75
- task_weights: bfloat16 [2, 4096, 16384], P('task', None, 'shard'), may hold values from -6 to 6
- example_count: int32 [2], P('task'), may hold values from 3 to 8, as said below
- example_start: int32 [2, 8], P('task'), may hold values from 0 to 1023, as said below
- example_len: int32 [2, 8], P('task'), may hold values from 1 to 128, as said below
Outputs:
- merged: bfloat16 [4096, 16384], P('task', 'shard')
The draws below stay inside these ranges and needn't reach their ends.
Inputs may be any that keep to these rules, and one draw needn't show every extreme that they name: Task t's examples are counted in slots 0 to example_count[t] - 1; some task has 8. Slot e of every task lies in rows e * 128 to (e + 1) * 128 - 1: example_start[t, e] >= e * 128 and example_start[t, e] + example_len[t, e] <= (e + 1) * 128. `example_len`: every task has a counted slot of exactly 128 rows.
All inputs are finite; a program needn't handle non-finite values.
Results may differ from the reference program's by a relative error of at most 0.007.
Values may be sent and summed in bfloat16 or wider, within the bound.
No kernel may reach another device: no remote copies, remote signals or barrier semaphores. Data moves between devices by JAX's collectives and lax.ppermute only.
A program may use at most 128 MiB of HBM per device.

```python
import jax
import jax.numpy as jnp
from jax import lax

D = 4096
FF = 16384
EX = 8
MOST = 128
TASKS = 2
TOKENS = 1024


def example_table(key):
    base = jax.random.fold_in(key, 9173)
    key_count, key_len, key_start, key_top, key_long = jax.random.split(base, 5)
    lowest = (EX + 2) // 3
    count = jax.random.randint(key_count, (TASKS,), lowest, EX + 1)
    top_task = jax.random.randint(key_top, (), 0, TASKS)
    count = jnp.where(jnp.arange(TASKS) == top_task, EX, count).astype(jnp.int32)
    lengths = jax.random.randint(key_len, (TASKS, EX), 1, MOST + 1)
    long_slot = jax.random.randint(key_long, (TASKS,), 0, count)
    slots = jnp.arange(EX, dtype=jnp.int32)
    lengths = jnp.where(slots[None, :] == long_slot[:, None], MOST, lengths).astype(jnp.int32)
    offset = jax.random.randint(key_start, (TASKS, EX), 0, MOST + 1 - lengths)
    starts = (slots[None, :] * MOST + offset).astype(jnp.int32)
    return (count, starts, lengths)


def draw_example_count(key, part):
    return example_table(key)[0]


def draw_example_start(key, part):
    return example_table(key)[1]


def draw_example_len(key, part):
    return example_table(key)[2]


def steps_of(key, dims, cuts, low, top_value):
    gain, own = 1.0, jax.random.fold_in(key, 6)
    for axis_at, shards_of in cuts:
        draws = jnp.exp(jax.random.uniform(jax.random.fold_in(own, axis_at), (shards_of,), jnp.float32, low / len(cuts), top_value / len(cuts)))
        gain = gain * jnp.repeat(draws, dims[axis_at] // shards_of).reshape([-1 if axis == axis_at else 1 for axis in range(len(dims))])
    return gain


def bell_draw(own_key, shape, width, bound, pieces=(), kind=jnp.bfloat16):
    values = jax.random.normal(own_key, shape, jnp.float32) * width
    if len(pieces) > 0:
        values = steps_of(own_key, shape, pieces, -0.22, 0.18) * values
    return jnp.clip(values, min=-bound, max=bound).astype(kind)


def setup_inputs(seed: int = 0) -> dict:
    keys = jax.random.split(jax.random.key(seed), 7)
    acts = bell_draw(keys[0], (TASKS, TOKENS, D), 1.0, 6.0, ((0, 2), (1, 16)))
    cotangents = bell_draw(keys[1], (TASKS, TOKENS, FF), 0.125, 0.75, ((0, 2), (1, 16)))
    task_weights = bell_draw(keys[2], (TASKS, D, FF), 1.0, 6.0, ((0, 2), (2, 16)))
    example_count = draw_example_count(jax.random.fold_in(keys[6], 71), 0)
    example_start = draw_example_start(jax.random.fold_in(keys[6], 71), 0)
    example_len = draw_example_len(jax.random.fold_in(keys[6], 71), 0)
    return {"acts": acts, "cotangents": cotangents, "task_weights": task_weights, "example_count": example_count, "example_start": example_start, "example_len": example_len}


def task_fisher(rows, grads, count, starts, lengths):
    def one_slot(slot, total):
        block_x = lax.dynamic_slice_in_dim(rows, slot * MOST, MOST, 0)
        block_g = lax.dynamic_slice_in_dim(grads, slot * MOST, MOST, 0)
        position = slot * MOST + jnp.arange(MOST, dtype=jnp.int32)
        first = starts[slot]
        keep = (position >= first) & (position < first + lengths[slot]) & (slot < count)
        masked = jnp.where(keep[:, None], block_g, jnp.zeros_like(block_g))
        grad = jnp.dot(block_x.T, masked, preferred_element_type=jnp.float32)
        return total + grad * grad
    total = lax.fori_loop(0, EX, one_slot, jnp.zeros((D, FF), jnp.float32))
    return (total / count.astype(jnp.float32)).astype(jnp.bfloat16)


def reference(acts, cotangents, task_weights, example_count, example_start, example_len):
    numer = jnp.zeros((D, FF), jnp.float32)
    denom = jnp.zeros((D, FF), jnp.float32)
    for task in range(TASKS):
        fisher = task_fisher(acts[task], cotangents[task], example_count[task], example_start[task], example_len[task])
        weight_f = fisher.astype(jnp.float32)
        numer = numer + weight_f * task_weights[task].astype(jnp.float32)
        denom = denom + weight_f
    return (numer / (denom + 1e-6)).astype(jnp.bfloat16)
```

```python
import functools

import jax
import jax.numpy as jnp
from jax import lax
from jax.experimental import pallas as pl
from jax.experimental.pallas import tpu as pltpu
from jax.sharding import PartitionSpec as P


def tile(size, most):
    part = size
    while part > most and part % 2 == 0:
        part //= 2
    return part


def fisher_rows(table_ref, task, x_ref, g_ref, slots, columns):
    devices, _, rows_each, width = x_ref.shape
    per_slot = rows_each * devices // slots
    spread = devices // slots
    total = None
    for slot in range(slots):
        x = x_ref[slot * spread : (slot + 1) * spread, 0].reshape(per_slot, width)
        row = slot * per_slot + lax.broadcasted_iota(jnp.int32, (per_slot, width), 0)
        first = table_ref[task, 1 + slot]
        last = first + table_ref[task, 1 + slots + slot]
        keep = (row >= first) & (row < last) & (slot < table_ref[task, 0])
        x = x * keep.astype(jnp.float32).astype(x.dtype)
        g = g_ref[slot * per_slot : (slot + 1) * per_slot, columns]
        grad = lax.dot_general(x, g, (((0,), (0,)), ((), ())), preferred_element_type=jnp.float32)
        total = grad * grad if total is None else total + grad * grad
    return (total / table_ref[task, 0].astype(jnp.float32)).astype(jnp.bfloat16)


def merge_kernel(tasks, slots, part, table_ref, *refs):
    x_refs, g_refs = refs[:tasks], refs[tasks : 2 * tasks]
    w_refs, out_ref = refs[2 * tasks : 3 * tasks], refs[3 * tasks]
    for start in range(0, out_ref.shape[1], part):
        columns = slice(start, start + part)
        numer, denom = None, None
        for task in range(tasks):
            fisher = fisher_rows(table_ref, task, x_refs[task], g_refs[task], slots, columns)
            fisher = fisher.astype(jnp.float32)
            term = fisher * w_refs[task][:, columns].astype(jnp.float32)
            numer = term if numer is None else numer + term
            denom = fisher if denom is None else denom + fisher
        out_ref[:, columns] = (numer / (denom + 1e-6)).astype(out_ref.dtype)


def per_device(tasks, acts, cotangents, task_weights, example_count, example_start, example_len):
    slots = example_start.shape[1]
    mine = lax.axis_index("task")
    high = acts.shape[2] // tasks
    width = task_weights.shape[2]
    tokens_each = acts.shape[1]

    def hand_on(step, value):
        return lax.ppermute(value, "task", [(i, (i + step) % tasks) for i in range(tasks)])

    def target(step):
        return lax.rem(mine + step, tasks)

    own = jnp.concatenate([example_count, example_start[0], example_len[0]])
    table = jnp.stack([own] + [hand_on(step, own) for step in range(1, tasks)])

    x_parts = []
    for step in range(tasks):
        part = lax.dynamic_slice_in_dim(acts[0], target(step) * high, high, 1)
        x_parts.append(part if step == 0 else hand_on(step, part))
    x = lax.all_gather(jnp.stack(x_parts), "shard", axis=0)

    grads = lax.all_to_all(cotangents[0], "shard", split_axis=1, concat_axis=0, tiled=True)
    g = [grads] + [hand_on(step, grads) for step in range(1, tasks)]

    w = []
    for step in range(tasks):
        part = lax.dynamic_slice_in_dim(task_weights[0], target(step) * high, high, 0)
        w.append(part if step == 0 else hand_on(step, part))

    block = tile(high, 256)
    devices = x.shape[0]
    x_specs = [
        pl.BlockSpec((devices, 1, tokens_each, block), functools.partial(lambda t, i, s: (0, t, 0, i), t))
        for t in range(tasks)
    ]
    g_specs = [pl.BlockSpec(grads.shape, lambda i, s: (0, 0)) for _ in range(tasks)]
    w_spec = pl.BlockSpec((block, width), lambda i, s: (i, 0))
    return pl.pallas_call(
        functools.partial(merge_kernel, tasks, slots, tile(width, 256)),
        out_shape=jax.ShapeDtypeStruct((high, width), jnp.bfloat16),
        grid_spec=pltpu.PrefetchScalarGridSpec(
            num_scalar_prefetch=1,
            grid=(high // block,),
            in_specs=x_specs + g_specs + [w_spec] * tasks,
            out_specs=w_spec,
        ),
        compiler_params=pltpu.CompilerParams(vmem_limit_bytes=48 * 1024 * 1024),
    )(table, *([x] * tasks), *g, *w)


def solution(mesh):
    in_specs = (
        P("task", "shard", None),
        P("task", "shard", None),
        P("task", None, "shard"),
        P("task"),
        P("task", None),
        P("task", None),
    )
    return jax.shard_map(
        functools.partial(per_device, mesh.shape["task"]),
        mesh=mesh,
        in_specs=in_specs,
        out_specs=P("task", "shard"),
        check_vma=False,
    )
```

```python
import functools

import jax
import jax.numpy as jnp
from jax import lax
from jax.experimental import pallas as pl
from jax.experimental.pallas import tpu as pltpu
from jax.sharding import PartitionSpec as P


def tile(size, most):
    part = size
    while part > most and part % 2 == 0:
        part //= 2
    return part


def fisher_rows(table_ref, task, x_ref, g_ref, slots, columns):
    devices, _, rows_each, width = x_ref.shape
    per_slot = rows_each * devices // slots
    spread = devices // slots
    total = None
    for slot in range(slots):
        x = x_ref[slot * spread : (slot + 1) * spread, 0].reshape(per_slot, width)
        g = g_ref[slot * per_slot : (slot + 1) * per_slot, columns]
        grad = lax.dot_general(x, g, (((0,), (0,)), ((), ())), preferred_element_type=jnp.float32)
        total = grad * grad if total is None else total + grad * grad
    return (total / table_ref[task, 0].astype(jnp.float32)).astype(jnp.bfloat16)


def fisher_kernel(task, slots, part, table_ref, x_ref, g_ref, out_ref):
    for start in range(0, out_ref.shape[1], part):
        columns = slice(start, start + part)
        out_ref[:, columns] = fisher_rows(table_ref, task, x_ref, g_ref, slots, columns)


def fisher_of(task, slots, table, x, g, high):
    devices, _, tokens_each, _ = x.shape
    width = g.shape[1]
    block = tile(high, 512)
    return pl.pallas_call(
        functools.partial(fisher_kernel, task, slots, tile(width, 256)),
        out_shape=jax.ShapeDtypeStruct((high, width), jnp.bfloat16),
        grid_spec=pltpu.PrefetchScalarGridSpec(
            num_scalar_prefetch=1,
            grid=(high // block,),
            in_specs=[
                pl.BlockSpec((devices, 1, tokens_each, block), lambda i, s: (0, task, 0, i)),
                pl.BlockSpec(g.shape, lambda i, s: (0, 0)),
            ],
            out_specs=pl.BlockSpec((block, width), lambda i, s: (i, 0)),
        ),
        compiler_params=pltpu.CompilerParams(vmem_limit_bytes=40 * 1024 * 1024),
        cost_estimate=pl.CostEstimate(
            flops=4 * high * width * g.shape[0], bytes_accessed=2 * high * width, transcendentals=0
        ),
    )(table, x, g)


def merge_kernel(tasks, slots, part, table_ref, *refs):
    f_ref, x_refs, g_refs = refs[0], refs[1:tasks], refs[tasks : 2 * tasks - 1]
    w_refs, out_ref = refs[2 * tasks - 1 : 3 * tasks - 1], refs[-1]
    for start in range(0, out_ref.shape[1], part):
        columns = slice(start, start + part)
        numer, denom = None, None
        for task in range(tasks):
            if task == 0:
                fisher = f_ref[:, columns]
            else:
                fisher = fisher_rows(table_ref, task, x_refs[task - 1], g_refs[task - 1], slots, columns)
            fisher = fisher.astype(jnp.float32)
            term = fisher * w_refs[task][:, columns].astype(jnp.float32)
            numer = term if numer is None else numer + term
            denom = fisher if denom is None else denom + fisher
        out_ref[:, columns] = (numer / (denom + 1e-6)).astype(out_ref.dtype)


def merge_columns(piece, slots, table, fisher, x, g, own, others, merged):
    tasks = 1 + len(others)
    devices, _, tokens_each, _ = x.shape
    high, width = fisher.shape
    some = g[0].shape[1]
    block = tile(high, 512)
    here = pl.BlockSpec((block, some), lambda i, s: (i, piece))
    own_spec = pl.BlockSpec((block, some), lambda i, s: (s[0, s.shape[1] - 1] * (high // block) + i, piece))
    x_specs = [
        pl.BlockSpec((devices, 1, tokens_each, block), functools.partial(lambda t, i, s: (0, t, 0, i), t))
        for t in range(1, tasks)
    ]
    g_specs = [pl.BlockSpec(part.shape, lambda i, s: (0, 0)) for part in g]
    in_specs = [here, *x_specs, *g_specs, own_spec] + [here] * (tasks - 1)
    operands = [table, fisher, *([x] * (tasks - 1)), *g, own, *others]
    aliases = {}
    if merged is not None:
        aliases = {len(operands): 0}
        in_specs.append(pl.BlockSpec(memory_space=pl.ANY))
        operands.append(merged)
    return pl.pallas_call(
        functools.partial(merge_kernel, tasks, slots, tile(some, 256)),
        out_shape=jax.ShapeDtypeStruct((high, width), jnp.bfloat16),
        grid_spec=pltpu.PrefetchScalarGridSpec(
            num_scalar_prefetch=1, grid=(high // block,), in_specs=in_specs, out_specs=here
        ),
        input_output_aliases=aliases,
        compiler_params=pltpu.CompilerParams(vmem_limit_bytes=40 * 1024 * 1024),
        cost_estimate=pl.CostEstimate(
            flops=4 * (tasks - 1) * high * some * g[0].shape[0],
            bytes_accessed=2 * (2 * tasks + 1) * high * some,
            transcendentals=0,
        ),
    )(*operands)


PIECES = 4
LANES = 128


def keep_rows(rows, count, starts, lengths):
    row = lax.axis_index("shard") * rows.shape[0] + jnp.arange(rows.shape[0], dtype=jnp.int32)[:, None]
    slot = jnp.arange(starts.shape[0], dtype=jnp.int32)
    keep = jnp.any((row >= starts) & (row < starts + lengths) & (slot < count), axis=1)
    return jnp.where(keep[:, None], rows, jnp.zeros_like(rows))


def per_device(tasks, acts, cotangents, task_weights, example_count, example_start, example_len):
    slots = example_start.shape[1]
    mine = lax.axis_index("task")
    high = acts.shape[2] // tasks
    steps = range(1, tasks)

    def hand_on(step, value):
        return lax.ppermute(value, "task", [(i, (i + step) % tasks) for i in range(tasks)])

    def block_of(step, value, axis):
        return lax.dynamic_slice_in_dim(value, lax.rem(mine + step, tasks) * high, high, axis)

    own = jnp.concatenate([example_count, mine[None]])
    table = jnp.stack([own] + [hand_on(step, own) for step in steps])

    kept = keep_rows(acts[0], example_count, example_start[0], example_len[0])
    x_parts = [block_of(0, kept, 1)] + [hand_on(step, block_of(step, kept, 1)) for step in steps]
    x = lax.all_gather(jnp.stack(x_parts), "shard", axis=0)
    others = [hand_on(step, block_of(step, task_weights[0], 0)) for step in steps]
    grads = lax.all_to_all(cotangents[0], "shard", split_axis=1, concat_axis=0, tiled=True)
    ready, others = lax.optimization_barrier((grads, others))
    count = max(1, min(PIECES, grads.shape[1] // LANES))
    some = grads.shape[1] // count
    pieces = [
        [hand_on(step, lax.slice_in_dim(ready, p * some, (p + 1) * some, axis=1)) for step in steps]
        for p in range(count)
    ]

    fisher = fisher_of(0, slots, table, x, grads, high)
    merged = None
    for piece in range(count):
        merged = merge_columns(
            piece, slots, table, fisher, x, pieces[piece], task_weights[0], others, merged
        )
    return merged


def solution(mesh):
    in_specs = (
        P("task", "shard", None),
        P("task", "shard", None),
        P("task", None, "shard"),
        P("task"),
        P("task", None),
        P("task", None),
    )
    return jax.shard_map(
        functools.partial(per_device, mesh.shape["task"]),
        mesh=mesh,
        in_specs=in_specs,
        out_specs=P("task", "shard"),
        check_vma=False,
    )
```

```python
import functools

import jax
import jax.numpy as jnp
from jax import lax
from jax.experimental import pallas as pl
from jax.experimental.pallas import tpu as pltpu
from jax.sharding import PartitionSpec as P


def tile(size, most):
    part = size
    while part > most and part % 2 == 0:
        part //= 2
    return part


def fisher_rows(table_ref, task, x_ref, g_ref, slots, columns):
    devices, _, rows_each, width = x_ref.shape
    per_slot = rows_each * devices // slots
    spread = devices // slots
    total = None
    for slot in range(slots):
        x = x_ref[slot * spread : (slot + 1) * spread, 0].reshape(per_slot, width)
        g = g_ref[slot * per_slot : (slot + 1) * per_slot, columns]
        grad = lax.dot_general(x, g, (((0,), (0,)), ((), ())), preferred_element_type=jnp.float32)
        total = grad * grad if total is None else total + grad * grad
    return (total / table_ref[task, 0].astype(jnp.float32)).astype(jnp.bfloat16)


def fisher_kernel(task, slots, part, table_ref, x_ref, g_ref, out_ref):
    for start in range(0, out_ref.shape[1], part):
        columns = slice(start, start + part)
        out_ref[:, columns] = fisher_rows(table_ref, task, x_ref, g_ref, slots, columns)


def fisher_of(task, slots, table, x, g, high):
    devices, _, tokens_each, _ = x.shape
    width = g.shape[1]
    block = tile(high, 512)
    return pl.pallas_call(
        functools.partial(fisher_kernel, task, slots, tile(width, 256)),
        out_shape=jax.ShapeDtypeStruct((high, width), jnp.bfloat16),
        grid_spec=pltpu.PrefetchScalarGridSpec(
            num_scalar_prefetch=1,
            grid=(high // block,),
            in_specs=[
                pl.BlockSpec((devices, 1, tokens_each, block), lambda i, s: (0, 0, 0, i)),
                pl.BlockSpec(g.shape, lambda i, s: (0, 0)),
            ],
            out_specs=pl.BlockSpec((block, width), lambda i, s: (i, 0)),
        ),
        compiler_params=pltpu.CompilerParams(vmem_limit_bytes=40 * 1024 * 1024),
        cost_estimate=pl.CostEstimate(
            flops=4 * high * width * g.shape[0], bytes_accessed=2 * high * width, transcendentals=0
        ),
    )(table, x, g)


def merge_kernel(tasks, slots, part, table_ref, *refs):
    f_ref, x_refs, g_refs = refs[0], refs[1:tasks], refs[tasks : 2 * tasks - 1]
    w_refs, out_ref = refs[2 * tasks - 1 : 3 * tasks - 1], refs[-1]
    for start in range(0, out_ref.shape[1], part):
        columns = slice(start, start + part)
        numer, denom = None, None
        for task in range(tasks):
            if task == 0:
                fisher = f_ref[:, columns]
            else:
                fisher = fisher_rows(table_ref, task, x_refs[task - 1], g_refs[task - 1], slots, columns)
            fisher = fisher.astype(jnp.float32)
            term = fisher * w_refs[task][:, columns].astype(jnp.float32)
            numer = term if numer is None else numer + term
            denom = fisher if denom is None else denom + fisher
        out_ref[:, columns] = (numer / (denom + 1e-6)).astype(out_ref.dtype)


def merge_columns(piece, slots, table, fisher, x, g, own, others, merged):
    tasks = 1 + len(others)
    devices, _, tokens_each, _ = x[0].shape
    high, width = fisher.shape
    some = g[0].shape[1]
    block = tile(high, 512)
    here = pl.BlockSpec((block, some), lambda i, s: (i, piece))
    own_spec = pl.BlockSpec((block, some), lambda i, s: (s[0, s.shape[1] - 1] * (high // block) + i, piece))
    x_specs = [
        pl.BlockSpec((devices, 1, tokens_each, block), lambda i, s: (0, 0, 0, i)) for _ in range(1, tasks)
    ]
    g_specs = [pl.BlockSpec(part.shape, lambda i, s: (0, 0)) for part in g]
    in_specs = [here, *x_specs, *g_specs, own_spec] + [here] * (tasks - 1)
    operands = [table, fisher, *x, *g, own, *others]
    aliases = {}
    if merged is not None:
        aliases = {len(operands): 0}
        in_specs.append(pl.BlockSpec(memory_space=pl.ANY))
        operands.append(merged)
    return pl.pallas_call(
        functools.partial(merge_kernel, tasks, slots, tile(some, 256)),
        out_shape=jax.ShapeDtypeStruct((high, width), jnp.bfloat16),
        grid_spec=pltpu.PrefetchScalarGridSpec(
            num_scalar_prefetch=1, grid=(high // block,), in_specs=in_specs, out_specs=here
        ),
        input_output_aliases=aliases,
        compiler_params=pltpu.CompilerParams(vmem_limit_bytes=40 * 1024 * 1024),
        cost_estimate=pl.CostEstimate(
            flops=4 * (tasks - 1) * high * some * g[0].shape[0],
            bytes_accessed=2 * (2 * tasks + 1) * high * some,
            transcendentals=0,
        ),
    )(*operands)


LANES = 128


def piece_bounds(width):
    half, quarter = width // 2, width // 4
    if quarter % LANES == 0:
        return [(0, half), (half, half + quarter), (half + quarter, width)]
    return [(0, half), (half, width)] if half % LANES == 0 else [(0, width)]


def keep_rows(rows, count, starts, lengths):
    row = lax.axis_index("shard") * rows.shape[0] + jnp.arange(rows.shape[0], dtype=jnp.int32)[:, None]
    slot = jnp.arange(starts.shape[0], dtype=jnp.int32)
    keep = jnp.any((row >= starts) & (row < starts + lengths) & (slot < count), axis=1)
    return jnp.where(keep[:, None], rows, jnp.zeros_like(rows))


def per_device(tasks, acts, cotangents, task_weights, example_count, example_start, example_len):
    slots = example_start.shape[1]
    mine = lax.axis_index("task")
    high = acts.shape[2] // tasks
    steps = range(1, tasks)

    def hand_on(step, value):
        return lax.ppermute(value, "task", [(i, (i + step) % tasks) for i in range(tasks)])

    def block_of(step, value, axis):
        return lax.dynamic_slice_in_dim(value, lax.rem(mine + step, tasks) * high, high, axis)

    own = jnp.concatenate([example_count, mine[None]])
    table = jnp.stack([own] + [hand_on(step, own) for step in steps])

    kept = keep_rows(acts[0], example_count, example_start[0], example_len[0])
    x_parts = [block_of(0, kept, 1)] + [hand_on(step, block_of(step, kept, 1)) for step in steps]
    x = [lax.all_gather(part[None], "shard", axis=0) for part in x_parts]
    others = [hand_on(step, block_of(step, task_weights[0], 0)) for step in steps]
    width = task_weights.shape[2]
    blocks = jnp.stack([cotangents[0][:, i : i + width] for i in range(0, cotangents.shape[2], width)])
    grads = lax.all_to_all(blocks, "shard", split_axis=0, concat_axis=0, tiled=True).reshape(-1, width)
    ready, others = lax.optimization_barrier((grads, others))
    bounds = piece_bounds(width)
    pieces = [
        [hand_on(step, lax.slice_in_dim(ready, low, top, axis=1)) for step in steps] for low, top in bounds
    ]

    fisher = fisher_of(0, slots, table, x[0], grads, high)
    merged = None
    for piece, (low, top) in enumerate(bounds):
        merged = merge_columns(
            low // (top - low), slots, table, fisher, x[1:], pieces[piece], task_weights[0], others, merged
        )
    return merged


def solution(mesh):
    in_specs = (
        P("task", "shard", None),
        P("task", "shard", None),
        P("task", None, "shard"),
        P("task"),
        P("task", None),
        P("task", None),
    )
    return jax.shard_map(
        functools.partial(per_device, mesh.shape["task"]),
        mesh=mesh,
        in_specs=in_specs,
        out_specs=P("task", "shard"),
        check_vma=False,
    )
```

```python
import functools

import jax
import jax.numpy as jnp
from jax import lax
from jax.experimental import pallas as pl
from jax.experimental.pallas import tpu as pltpu
from jax.sharding import PartitionSpec as P


def tile(size, most):
    part = size
    while part > most and part % 2 == 0:
        part //= 2
    return part


def fisher_rows(table_ref, task, x_ref, g_ref, slots, columns):
    devices, _, rows_each, width = x_ref.shape
    per_slot = rows_each * devices // slots
    spread = devices // slots
    total = None
    for slot in range(slots):
        x = x_ref[slot * spread : (slot + 1) * spread, 0].reshape(per_slot, width)
        g = g_ref[slot * per_slot : (slot + 1) * per_slot, columns]
        grad = lax.dot_general(x, g, (((0,), (0,)), ((), ())), preferred_element_type=jnp.float32)
        total = grad * grad if total is None else total + grad * grad
    return (total / table_ref[task, 0].astype(jnp.float32)).astype(jnp.bfloat16)


def fisher_kernel(task, slots, part, table_ref, x_ref, g_ref, out_ref):
    for start in range(0, out_ref.shape[1], part):
        columns = slice(start, start + part)
        out_ref[:, columns] = fisher_rows(table_ref, task, x_ref, g_ref, slots, columns)


def fisher_of(task, slots, table, x, g, high):
    devices, _, tokens_each, _ = x.shape
    width = g.shape[1]
    block = tile(high, 512)
    return pl.pallas_call(
        functools.partial(fisher_kernel, task, slots, tile(width, 256)),
        out_shape=jax.ShapeDtypeStruct((high, width), jnp.bfloat16),
        grid_spec=pltpu.PrefetchScalarGridSpec(
            num_scalar_prefetch=1,
            grid=(high // block,),
            in_specs=[
                pl.BlockSpec((devices, 1, tokens_each, block), lambda i, s: (0, 0, 0, i)),
                pl.BlockSpec(g.shape, lambda i, s: (0, 0)),
            ],
            out_specs=pl.BlockSpec((block, width), lambda i, s: (i, 0)),
        ),
        compiler_params=pltpu.CompilerParams(vmem_limit_bytes=40 * 1024 * 1024),
        cost_estimate=pl.CostEstimate(
            flops=4 * high * width * g.shape[0], bytes_accessed=2 * high * width, transcendentals=0
        ),
    )(table, x, g)


def merge_kernel(tasks, slots, part, joined, table_ref, *refs):
    f_ref, x_refs, refs = refs[0], refs[1:tasks], refs[tasks:]
    g_refs, refs = refs[: joined * (tasks - 1)], refs[joined * (tasks - 1) :]
    w_refs, out_ref = refs[:tasks], refs[-1]
    where = [(i, at) for i in range(joined) for at in range(0, g_refs[i].shape[1], part)]
    for start in range(0, out_ref.shape[1], part):
        columns = slice(start, start + part)
        numer, denom = None, None
        for task in range(tasks):
            if task == 0:
                fisher = f_ref[:, columns]
            else:
                piece, at = where[start // part]
                g_ref = g_refs[(task - 1) * joined + piece]
                fisher = fisher_rows(table_ref, task, x_refs[task - 1], g_ref, slots, slice(at, at + part))
            fisher = fisher.astype(jnp.float32)
            term = fisher * w_refs[task][:, columns].astype(jnp.float32)
            numer = term if numer is None else numer + term
            denom = fisher if denom is None else denom + fisher
        out_ref[:, columns] = (numer / (denom + 1e-6)).astype(out_ref.dtype)


def merge_columns(piece, slots, table, fisher, x, g, own, others, merged):
    tasks = 1 + len(others)
    devices, _, tokens_each, _ = x[0].shape
    high, width = fisher.shape
    joined = len(g) // (tasks - 1)
    some = sum(part.shape[1] for part in g[:joined])
    block = tile(high, 512)
    here = pl.BlockSpec((block, some), lambda i, s: (i, piece))
    own_spec = pl.BlockSpec((block, some), lambda i, s: (s[0, s.shape[1] - 1] * (high // block) + i, piece))
    x_specs = [
        pl.BlockSpec((devices, 1, tokens_each, block), lambda i, s: (0, 0, 0, i)) for _ in range(1, tasks)
    ]
    g_specs = [pl.BlockSpec(part.shape, lambda i, s: (0, 0)) for part in g]
    in_specs = [here, *x_specs, *g_specs, own_spec] + [here] * (tasks - 1)
    operands = [table, fisher, *x, *g, own, *others]
    aliases = {}
    if merged is not None:
        aliases = {len(operands): 0}
        in_specs.append(pl.BlockSpec(memory_space=pl.ANY))
        operands.append(merged)
    return pl.pallas_call(
        functools.partial(merge_kernel, tasks, slots, min(tile(part.shape[1], 256) for part in g), joined),
        out_shape=jax.ShapeDtypeStruct((high, width), jnp.bfloat16),
        grid_spec=pltpu.PrefetchScalarGridSpec(
            num_scalar_prefetch=1, grid=(high // block,), in_specs=in_specs, out_specs=here
        ),
        input_output_aliases=aliases,
        compiler_params=pltpu.CompilerParams(vmem_limit_bytes=60 * 1024 * 1024),
        cost_estimate=pl.CostEstimate(
            flops=4 * (tasks - 1) * high * some * g[0].shape[0],
            bytes_accessed=2 * (2 * tasks + 1) * high * some,
            transcendentals=0,
        ),
    )(*operands)


LANES = 128


def piece_bounds(width):
    half, quarter = width // 2, width // 4
    if quarter % LANES == 0:
        return [(0, half), (half, half + quarter), (half + quarter, width)]
    return [(0, half), (half, width)] if half % LANES == 0 else [(0, width)]


def keep_rows(rows, count, starts, lengths):
    row = lax.axis_index("shard") * rows.shape[0] + jnp.arange(rows.shape[0], dtype=jnp.int32)[:, None]
    slot = jnp.arange(starts.shape[0], dtype=jnp.int32)
    keep = jnp.any((row >= starts) & (row < starts + lengths) & (slot < count), axis=1)
    return jnp.where(keep[:, None], rows, jnp.zeros_like(rows))


def per_device(tasks, acts, cotangents, task_weights, example_count, example_start, example_len):
    slots = example_start.shape[1]
    mine = lax.axis_index("task")
    high = acts.shape[2] // tasks
    steps = range(1, tasks)

    def hand_on(step, value):
        return lax.ppermute(value, "task", [(i, (i + step) % tasks) for i in range(tasks)])

    def block_of(step, value, axis):
        return lax.dynamic_slice_in_dim(value, lax.rem(mine + step, tasks) * high, high, axis)

    own = jnp.concatenate([example_count, mine[None]])
    table = jnp.stack([own] + [hand_on(step, own) for step in steps])

    kept = keep_rows(acts[0], example_count, example_start[0], example_len[0])
    x_parts = [block_of(0, kept, 1)] + [hand_on(step, block_of(step, kept, 1)) for step in steps]
    x = [lax.all_gather(part[None], "shard", axis=0) for part in x_parts]
    others = [hand_on(step, block_of(step, task_weights[0], 0)) for step in steps]
    width = task_weights.shape[2]
    blocks = jnp.stack([cotangents[0][:, i : i + width] for i in range(0, cotangents.shape[2], width)])
    grads = lax.all_to_all(blocks, "shard", split_axis=0, concat_axis=0, tiled=True).reshape(-1, width)
    ready, others = lax.optimization_barrier((grads, others))
    bounds = piece_bounds(width)
    pieces = [
        [hand_on(step, lax.slice_in_dim(ready, low, top, axis=1)) for step in steps] for low, top in bounds
    ]

    fisher = fisher_of(0, slots, table, x[0], grads, high)
    merged = None
    groups = [range(0, 2), range(2, 3)] if len(bounds) == 3 else [[p] for p in range(len(bounds))]
    for group in groups:
        low, top = bounds[group[0]][0], bounds[group[-1]][1]
        g = [pieces[p][step - 1] for step in steps for p in group]
        merged = merge_columns(
            low // (top - low), slots, table, fisher, x[1:], g, task_weights[0], others, merged
        )
    return merged


def solution(mesh):
    in_specs = (
        P("task", "shard", None),
        P("task", "shard", None),
        P("task", None, "shard"),
        P("task"),
        P("task", None),
        P("task", None),
    )
    return jax.shard_map(
        functools.partial(per_device, mesh.shape["task"]),
        mesh=mesh,
        in_specs=in_specs,
        out_specs=P("task", "shard"),
        check_vma=False,
    )
```

```python
import functools

import jax
import jax.numpy as jnp
from jax import lax
from jax.experimental import pallas as pl
from jax.experimental.pallas import tpu as pltpu
from jax.sharding import PartitionSpec as P


def tile(size, most):
    part = size
    while part > most and part % 2 == 0:
        part //= 2
    return part


def fisher_tile(table_ref, task, x_ref, g_ref, slots, lanes, columns):
    devices, _, rows_each, _ = x_ref.shape
    per_slot = rows_each * devices // slots
    spread = devices // slots
    total = None
    for slot in range(slots):
        x = x_ref[slot * spread : (slot + 1) * spread, 0, :, lanes]
        x = x.reshape(per_slot, x.shape[-1])
        g = g_ref[slot * per_slot : (slot + 1) * per_slot, columns]
        grad = lax.dot_general(x, g, (((0,), (0,)), ((), ())), preferred_element_type=jnp.float32)
        total = grad * grad if total is None else total + grad * grad
    return (total / table_ref[task, 0].astype(jnp.float32)).astype(jnp.bfloat16)


def fisher_rows(table_ref, task, x_ref, g_ref, slots, columns):
    width = x_ref.shape[3]
    some = tile(width, 128)
    parts = [
        fisher_tile(table_ref, task, x_ref, g_ref, slots, slice(low, low + some), columns)
        for low in range(0, width, some)
    ]
    return jnp.concatenate(parts, axis=0)


def fisher_kernel(task, slots, part, table_ref, x_ref, g_ref, out_ref):
    for start in range(0, out_ref.shape[1], part):
        columns = slice(start, start + part)
        out_ref[:, columns] = fisher_rows(table_ref, task, x_ref, g_ref, slots, columns)


def fisher_of(task, slots, table, x, g, high):
    devices, _, tokens_each, _ = x.shape
    width = g.shape[1]
    block = tile(high, 512)
    return pl.pallas_call(
        functools.partial(fisher_kernel, task, slots, tile(width, 256)),
        out_shape=jax.ShapeDtypeStruct((high, width), jnp.bfloat16),
        grid_spec=pltpu.PrefetchScalarGridSpec(
            num_scalar_prefetch=1,
            grid=(high // block,),
            in_specs=[
                pl.BlockSpec((devices, 1, tokens_each, block), lambda i, s: (0, 0, 0, i)),
                pl.BlockSpec(g.shape, lambda i, s: (0, 0)),
            ],
            out_specs=pl.BlockSpec((block, width), lambda i, s: (i, 0)),
        ),
        compiler_params=pltpu.CompilerParams(vmem_limit_bytes=40 * 1024 * 1024),
        cost_estimate=pl.CostEstimate(
            flops=4 * high * width * g.shape[0], bytes_accessed=2 * high * width, transcendentals=0
        ),
    )(table, x, g)


def merge_kernel(tasks, slots, part, joined, table_ref, *refs):
    f_ref, x_refs, refs = refs[0], refs[1:tasks], refs[tasks:]
    g_refs, refs = refs[: joined * (tasks - 1)], refs[joined * (tasks - 1) :]
    w_refs, out_ref = refs[:tasks], refs[-1]
    where = [(i, at) for i in range(joined) for at in range(0, g_refs[i].shape[1], part)]
    for start in range(0, out_ref.shape[1], part):
        columns = slice(start, start + part)
        numer, denom = None, None
        for task in range(tasks):
            if task == 0:
                fisher = f_ref[:, columns]
            else:
                piece, at = where[start // part]
                g_ref = g_refs[(task - 1) * joined + piece]
                fisher = fisher_rows(table_ref, task, x_refs[task - 1], g_ref, slots, slice(at, at + part))
            fisher = fisher.astype(jnp.float32)
            term = fisher * w_refs[task][:, columns].astype(jnp.float32)
            numer = term if numer is None else numer + term
            denom = fisher if denom is None else denom + fisher
        out_ref[:, columns] = (numer / (denom + 1e-6)).astype(out_ref.dtype)


def merge_columns(piece, slots, table, fisher, x, g, own, others, merged):
    tasks = 1 + len(others)
    devices, _, tokens_each, _ = x[0].shape
    high, width = fisher.shape
    joined = len(g) // (tasks - 1)
    some = sum(part.shape[1] for part in g[:joined])
    block = tile(high, 512 if joined > 1 else 1024)
    here = pl.BlockSpec((block, some), lambda i, s: (i, piece))
    own_spec = pl.BlockSpec((block, some), lambda i, s: (s[0, s.shape[1] - 1] * (high // block) + i, piece))
    x_specs = [
        pl.BlockSpec((devices, 1, tokens_each, block), lambda i, s: (0, 0, 0, i)) for _ in range(1, tasks)
    ]
    g_specs = [pl.BlockSpec(part.shape, lambda i, s: (0, 0)) for part in g]
    in_specs = [here, *x_specs, *g_specs, own_spec] + [here] * (tasks - 1)
    operands = [table, fisher, *x, *g, own, *others]
    aliases = {}
    if merged is not None:
        aliases = {len(operands): 0}
        in_specs.append(pl.BlockSpec(memory_space=pl.ANY))
        operands.append(merged)
    return pl.pallas_call(
        functools.partial(merge_kernel, tasks, slots, min(tile(part.shape[1], 256) for part in g), joined),
        out_shape=jax.ShapeDtypeStruct((high, width), jnp.bfloat16),
        grid_spec=pltpu.PrefetchScalarGridSpec(
            num_scalar_prefetch=1, grid=(high // block,), in_specs=in_specs, out_specs=here
        ),
        input_output_aliases=aliases,
        compiler_params=pltpu.CompilerParams(vmem_limit_bytes=60 * 1024 * 1024),
        cost_estimate=pl.CostEstimate(
            flops=4 * (tasks - 1) * high * some * g[0].shape[0],
            bytes_accessed=2 * (2 * tasks + 1) * high * some,
            transcendentals=0,
        ),
    )(*operands)


LANES = 128


def piece_bounds(width):
    half, quarter = width // 2, width // 4
    if quarter % LANES == 0:
        return [(0, half), (half, half + quarter), (half + quarter, width)]
    return [(0, half), (half, width)] if half % LANES == 0 else [(0, width)]


def keep_rows(rows, count, starts, lengths):
    row = lax.axis_index("shard") * rows.shape[0] + jnp.arange(rows.shape[0], dtype=jnp.int32)[:, None]
    slot = jnp.arange(starts.shape[0], dtype=jnp.int32)
    keep = jnp.any((row >= starts) & (row < starts + lengths) & (slot < count), axis=1)
    return jnp.where(keep[:, None], rows, jnp.zeros_like(rows))


def per_device(tasks, acts, cotangents, task_weights, example_count, example_start, example_len):
    slots = example_start.shape[1]
    mine = lax.axis_index("task")
    high = acts.shape[2] // tasks
    steps = range(1, tasks)

    def hand_on(step, value):
        return lax.ppermute(value, "task", [(i, (i + step) % tasks) for i in range(tasks)])

    def block_of(step, value, axis):
        return lax.dynamic_slice_in_dim(value, lax.rem(mine + step, tasks) * high, high, axis)

    own = jnp.concatenate([example_count, mine[None]])
    table = jnp.stack([own] + [hand_on(step, own) for step in steps])

    kept = keep_rows(acts[0], example_count, example_start[0], example_len[0])
    x_parts = [block_of(0, kept, 1)] + [hand_on(step, block_of(step, kept, 1)) for step in steps]
    x = [lax.all_gather(part[None], "shard", axis=0) for part in x_parts]
    others = [hand_on(step, block_of(step, task_weights[0], 0)) for step in steps]
    width = task_weights.shape[2]
    blocks = jnp.stack([cotangents[0][:, i : i + width] for i in range(0, cotangents.shape[2], width)])
    grads = lax.all_to_all(blocks, "shard", split_axis=0, concat_axis=0, tiled=True).reshape(-1, width)
    ready, others = lax.optimization_barrier((grads, others))
    bounds = piece_bounds(width)
    pieces = [
        [hand_on(step, lax.slice_in_dim(ready, low, top, axis=1)) for step in steps] for low, top in bounds
    ]

    fisher = fisher_of(0, slots, table, x[0], grads, high)
    merged = None
    groups = [range(0, 2), range(2, 3)] if len(bounds) == 3 else [[p] for p in range(len(bounds))]
    for group in groups:
        low, top = bounds[group[0]][0], bounds[group[-1]][1]
        g = [pieces[p][step - 1] for step in steps for p in group]
        merged = merge_columns(
            low // (top - low), slots, table, fisher, x[1:], g, task_weights[0], others, merged
        )
    return merged


def solution(mesh):
    in_specs = (
        P("task", "shard", None),
        P("task", "shard", None),
        P("task", None, "shard"),
        P("task"),
        P("task", None),
        P("task", None),
    )
    return jax.shard_map(
        functools.partial(per_device, mesh.shape["task"]),
        mesh=mesh,
        in_specs=in_specs,
        out_specs=P("task", "shard"),
        check_vma=False,
    )
```

```python
import functools

import jax
import jax.numpy as jnp
from jax import lax
from jax.experimental import pallas as pl
from jax.experimental.pallas import tpu as pltpu
from jax.sharding import PartitionSpec as P


def tile(size, most):
    part = size
    while part > most and part % 2 == 0:
        part //= 2
    return part


def fisher_tile(table_ref, task, x_ref, g_ref, slots, lanes, columns):
    devices, _, rows_each, _ = x_ref.shape
    per_slot = rows_each * devices // slots
    spread = devices // slots
    total = None
    for slot in range(slots):
        x = x_ref[slot * spread : (slot + 1) * spread, 0, :, lanes]
        x = x.reshape(per_slot, x.shape[-1])
        g = g_ref[slot * per_slot : (slot + 1) * per_slot, columns]
        grad = lax.dot_general(x, g, (((0,), (0,)), ((), ())), preferred_element_type=jnp.float32)
        total = grad * grad if total is None else total + grad * grad
    return (total / table_ref[task, 0].astype(jnp.float32)).astype(jnp.bfloat16)


def fisher_rows(table_ref, task, x_ref, g_ref, slots, columns):
    width = x_ref.shape[3]
    some = tile(width, 128)
    parts = [
        fisher_tile(table_ref, task, x_ref, g_ref, slots, slice(low, low + some), columns)
        for low in range(0, width, some)
    ]
    return jnp.concatenate(parts, axis=0)


def fisher_kernel(task, slots, part, table_ref, x_ref, g_ref, out_ref):
    for start in range(0, out_ref.shape[1], part):
        columns = slice(start, start + part)
        out_ref[:, columns] = fisher_rows(table_ref, task, x_ref, g_ref, slots, columns)


def fisher_of(task, slots, table, x, g, high):
    devices, _, tokens_each, _ = x.shape
    width = g.shape[1]
    block = tile(high, 512)
    return pl.pallas_call(
        functools.partial(fisher_kernel, task, slots, tile(width, 256)),
        out_shape=jax.ShapeDtypeStruct((high, width), jnp.bfloat16),
        grid_spec=pltpu.PrefetchScalarGridSpec(
            num_scalar_prefetch=1,
            grid=(high // block,),
            in_specs=[
                pl.BlockSpec((devices, 1, tokens_each, block), lambda i, s: (0, 0, 0, i)),
                pl.BlockSpec(g.shape, lambda i, s: (0, 0)),
            ],
            out_specs=pl.BlockSpec((block, width), lambda i, s: (i, 0)),
        ),
        compiler_params=pltpu.CompilerParams(vmem_limit_bytes=40 * 1024 * 1024),
        cost_estimate=pl.CostEstimate(
            flops=4 * high * width * g.shape[0], bytes_accessed=2 * high * width, transcendentals=0
        ),
    )(table, x, g)


def merge_kernel(tasks, slots, part, joined, table_ref, *refs):
    f_ref, x_refs, refs = refs[0], refs[1:tasks], refs[tasks:]
    g_refs, refs = refs[: joined * (tasks - 1)], refs[joined * (tasks - 1) :]
    w_refs, out_ref = refs[:tasks], refs[-1]
    where = [(i, at) for i in range(joined) for at in range(0, g_refs[i].shape[1], part)]
    for start in range(0, out_ref.shape[1], part):
        columns = slice(start, start + part)
        numer, denom = None, None
        for task in range(tasks):
            if task == 0:
                fisher = f_ref[:, columns]
            else:
                piece, at = where[start // part]
                g_ref = g_refs[(task - 1) * joined + piece]
                fisher = fisher_rows(table_ref, task, x_refs[task - 1], g_ref, slots, slice(at, at + part))
            fisher = fisher.astype(jnp.float32)
            term = fisher * w_refs[task][:, columns].astype(jnp.float32)
            numer = term if numer is None else numer + term
            denom = fisher if denom is None else denom + fisher
        out_ref[:, columns] = (numer / (denom + 1e-6)).astype(out_ref.dtype)


def merge_columns(piece, slots, table, fisher, x, g, own, others, merged):
    tasks = 1 + len(others)
    devices, _, tokens_each, _ = x[0].shape
    high, width = fisher.shape
    joined = len(g) // (tasks - 1)
    some = sum(part.shape[1] for part in g[:joined])
    block = tile(high, 1024)
    here = pl.BlockSpec((block, some), lambda i, s: (i, piece))
    own_spec = pl.BlockSpec((block, some), lambda i, s: (s[0, s.shape[1] - 1] * (high // block) + i, piece))
    x_specs = [
        pl.BlockSpec((devices, 1, tokens_each, block), lambda i, s: (0, 0, 0, i)) for _ in range(1, tasks)
    ]
    g_specs = [pl.BlockSpec(part.shape, lambda i, s: (0, 0)) for part in g]
    in_specs = [here, *x_specs, *g_specs, own_spec] + [here] * (tasks - 1)
    operands = [table, fisher, *x, *g, own, *others]
    aliases = {}
    if merged is not None:
        aliases = {len(operands): 0}
        in_specs.append(pl.BlockSpec(memory_space=pl.ANY))
        operands.append(merged)
    return pl.pallas_call(
        functools.partial(merge_kernel, tasks, slots, min(tile(part.shape[1], 256) for part in g), joined),
        out_shape=jax.ShapeDtypeStruct((high, width), jnp.bfloat16),
        grid_spec=pltpu.PrefetchScalarGridSpec(
            num_scalar_prefetch=1, grid=(high // block,), in_specs=in_specs, out_specs=here
        ),
        input_output_aliases=aliases,
        compiler_params=pltpu.CompilerParams(vmem_limit_bytes=60 * 1024 * 1024),
        cost_estimate=pl.CostEstimate(
            flops=4 * (tasks - 1) * high * some * g[0].shape[0],
            bytes_accessed=2 * (2 * tasks + 1) * high * some,
            transcendentals=0,
        ),
    )(*operands)


LANES = 128


def piece_bounds(width):
    half, quarter = width // 2, width // 4
    if quarter % LANES == 0:
        return [(0, half), (half, half + quarter), (half + quarter, width)]
    return [(0, half), (half, width)] if half % LANES == 0 else [(0, width)]


def keep_rows(rows, count, starts, lengths):
    row = lax.axis_index("shard") * rows.shape[0] + jnp.arange(rows.shape[0], dtype=jnp.int32)[:, None]
    slot = jnp.arange(starts.shape[0], dtype=jnp.int32)
    keep = jnp.any((row >= starts) & (row < starts + lengths) & (slot < count), axis=1)
    return jnp.where(keep[:, None], rows, jnp.zeros_like(rows))


def per_device(tasks, acts, cotangents, task_weights, example_count, example_start, example_len):
    slots = example_start.shape[1]
    mine = lax.axis_index("task")
    high = acts.shape[2] // tasks
    steps = range(1, tasks)

    def hand_on(step, value):
        return lax.ppermute(value, "task", [(i, (i + step) % tasks) for i in range(tasks)])

    def block_of(step, value, axis):
        return lax.dynamic_slice_in_dim(value, lax.rem(mine + step, tasks) * high, high, axis)

    own = jnp.concatenate([example_count, mine[None]])
    table = jnp.stack([own] + [hand_on(step, own) for step in steps])

    kept = keep_rows(acts[0], example_count, example_start[0], example_len[0])
    x_parts = [block_of(0, kept, 1)] + [hand_on(step, block_of(step, kept, 1)) for step in steps]
    x = [lax.all_gather(part[None], "shard", axis=0) for part in x_parts]
    others = [hand_on(step, block_of(step, task_weights[0], 0)) for step in steps]
    width = task_weights.shape[2]
    blocks = jnp.stack([cotangents[0][:, i : i + width] for i in range(0, cotangents.shape[2], width)])
    grads = lax.all_to_all(blocks, "shard", split_axis=0, concat_axis=0, tiled=True).reshape(-1, width)
    ready, others = lax.optimization_barrier((grads, others))
    bounds = piece_bounds(width)
    pieces = [
        [hand_on(step, lax.slice_in_dim(ready, low, top, axis=1)) for step in steps] for low, top in bounds
    ]

    fisher = fisher_of(0, slots, table, x[0], grads, high)
    merged = None
    groups = [range(0, 2), range(2, 3)] if len(bounds) == 3 else [[p] for p in range(len(bounds))]
    for group in groups:
        low, top = bounds[group[0]][0], bounds[group[-1]][1]
        g = [pieces[p][step - 1] for step in steps for p in group]
        merged = merge_columns(
            low // (top - low), slots, table, fisher, x[1:], g, task_weights[0], others, merged
        )
    return merged


def solution(mesh):
    in_specs = (
        P("task", "shard", None),
        P("task", "shard", None),
        P("task", None, "shard"),
        P("task"),
        P("task", None),
        P("task", None),
    )
    return jax.shard_map(
        functools.partial(per_device, mesh.shape["task"]),
        mesh=mesh,
        in_specs=in_specs,
        out_specs=P("task", "shard"),
        check_vma=False,
    )
```
